32 devices in a mesh: cuts: 8 (over y, x, core), pencil: 4 (over z).
Axes of the slice: x: 2, y: 2, z: 4, core: 2. Of those that a mesh axis runs over, the one named last changes fastest.
Arguments:
- wavefunctions: bfloat16 [32, 9216, 192], P('cuts', 'pencil'), may hold values from -8 to 8
- potential: float32 [192, 192, 192], P('pencil'), may hold values from -6 to 6
- keep_mask: int32 [8, 2, 2], P('cuts'), may hold values 0 or 1
- stick_map: int32 [9216], P('pencil'), may hold values from 0 to 2303, as said below
Outputs:
- hamiltonian_bands: bfloat16 [32, 9216, 192], P('cuts', 'pencil')
The draws below stay inside these ranges and needn't reach their ends.
Inputs may be any that keep to these rules, and one draw needn't show every extreme that they name: `stick_map`: each block of 2304 consecutive entries (one index of pencil) is a permutation of 0 to 2303.
All inputs are finite; a program needn't handle non-finite values. No bound on the sum of `keep_mask` on one device may be relied on, other than what follows from the above.
Results may differ from the reference program's by a relative error of at most 0.0065.
Values may be sent and summed in bfloat16 or wider, within the bound.
A program may use at most 256 MiB of HBM per device.

```python
import math
import jax
import jax.numpy as jnp
from jax import lax

GRID = 192
EDGE = 2
BANDS_DEV = 4
GBOX = 96
BANDS = 32
GY_DEV = 24
STICKS = 9216
STICKS_DEV = 2304
N_CUTS = 8


def fresh_noise(noise_key, band_index):
    band_key = jax.random.fold_in(noise_key, band_index)
    return jax.random.normal(band_key, (STICKS, 2 * GBOX), jnp.float32)


def draw_wavefunctions(key, part):
    blocks = STICKS // STICKS_DEV
    coef_key = jax.random.fold_in(key, 11)
    sign_key = jax.random.fold_in(key, 12)
    scale_key = jax.random.fold_in(key, 13)
    noise_key = jax.random.fold_in(key, 14)
    magnitudes = jax.random.uniform(coef_key, (BANDS, blocks), jnp.float32, 0.3, 0.95)
    signs = (2 * jax.random.randint(sign_key, (BANDS, blocks), 0, 2) - 1).astype(jnp.float32)
    coefficients = jnp.repeat(magnitudes * signs, STICKS_DEV, axis=1)
    block_scale = jnp.exp(jax.random.uniform(scale_key, (blocks,), jnp.float32, 0.0, math.log(3.0))) / math.sqrt(3.0)
    block_scale = jnp.repeat(block_scale, STICKS_DEV)

    def advance(previous, inputs):
        band_index, coef_row = inputs
        column = coef_row[:, None]
        following = column * previous + jnp.sqrt(1.0 - column * column) * fresh_noise(noise_key, band_index)
        return (following, following)
    start = fresh_noise(noise_key, BANDS)
    band_ids = jnp.arange(BANDS, dtype=jnp.int32)
    unused, mixture = lax.scan(advance, start, (band_ids, coefficients))
    mixture = mixture * block_scale[None, :, None]
    return jnp.clip(mixture, -8.0, 8.0).astype(jnp.bfloat16)


def draw_stick_map(key, part):
    owners = STICKS // STICKS_DEV
    key_list = jax.random.split(key, owners)
    orders = jax.vmap(lambda single: jax.random.permutation(single, STICKS_DEV))(key_list)
    return orders.reshape(STICKS).astype(jnp.int32)


def with_ends(drawn, key, least, high):
    longest = drawn.shape.index(max(drawn.shape))
    spots = []
    for shift in (0, 1):
        where = [jax.random.randint(jax.random.fold_in(key, axis), (), 0, length) for axis, length in enumerate(drawn.shape)]
        where[longest] = (where[longest] + shift) % drawn.shape[longest]
        spots.append(tuple(where))
    return drawn.at[spots[0]].set(least).at[spots[1]].set(high)


def shard_levels(stream_key, extent, cuts, low, high):
    factor_of, own = 1.0, jax.random.fold_in(stream_key, 6)
    for dim, shards_of in cuts:
        draws = jnp.exp(jax.random.uniform(jax.random.fold_in(own, dim), (shards_of,), jnp.float32, low / len(cuts), high / len(cuts)))
        factor_of = factor_of * jnp.repeat(draws, extent[dim] // shards_of).reshape([-1 if axis == dim else 1 for axis in range(len(extent))])
    return factor_of


def normal_values(key, shape, scale, limit, cuts=(), held_as=jnp.bfloat16):
    level = shard_levels(key, shape, cuts, -0.22, 0.18) if cuts else 1.0
    array = jax.random.normal(key, shape, jnp.float32) * scale * level
    return jnp.minimum(jnp.maximum(array, -limit), limit).astype(held_as)


def setup_inputs(seed: int = 0) -> dict:
    key_of = jax.random.split(jax.random.key(seed), 5)
    wavefunctions = draw_wavefunctions(jax.random.fold_in(key_of[4], 71), 0)
    potential = normal_values(key_of[1], (GRID, GRID, GRID), 1.0, 6.0, ((0, 4),), jnp.float32)
    keep_mask = with_ends((jax.random.randint(key_of[2], (N_CUTS, EDGE, EDGE), 0, 2) < 1).astype(jnp.int32), jax.random.fold_in(key_of[2], 1), 0, 1)
    stick_map = draw_stick_map(jax.random.fold_in(key_of[4], 71), 0)
    return {"wavefunctions": wavefunctions, "potential": potential, "keep_mask": keep_mask, "stick_map": stick_map}


def dft_tables(box_size, length):
    frequency = jnp.arange(box_size, dtype=jnp.float32) - float(box_size // 2)
    points = jnp.arange(length, dtype=jnp.float32)
    phases = 2.0 * math.pi / length * jnp.mod(frequency[:, None] * points[None, :], float(length))
    ahead_scale = 1.0 / math.sqrt(box_size)
    behind_scale = math.sqrt(box_size) / length
    ahead_cos = (jnp.cos(phases) * ahead_scale).astype(jnp.bfloat16)
    ahead_sin = (jnp.sin(phases) * ahead_scale).astype(jnp.bfloat16)
    behind_cos = (jnp.cos(phases).T * behind_scale).astype(jnp.bfloat16)
    behind_sin = (-jnp.sin(phases).T * behind_scale).astype(jnp.bfloat16)
    return (ahead_cos, ahead_sin, behind_cos, behind_sin)

def last_matrix(cos_table, sin_table):
    upper_rows = jnp.concatenate([cos_table, sin_table], axis=1)
    lower_rows = jnp.concatenate([-sin_table, cos_table], axis=1)
    return jnp.concatenate([upper_rows, lower_rows], axis=0)

def combine_halves(cos_part, sin_part):
    middle = cos_part.shape[-1] // 2
    real_part = cos_part[..., :middle] - sin_part[..., middle:]
    imag_part = sin_part[..., :middle] + cos_part[..., middle:]
    return jnp.concatenate([real_part, imag_part], axis=-1)

def along_axis(values, cos_table, sin_table, pattern):
    operand = values.astype(jnp.float32)
    cos_part = jnp.einsum(pattern, operand, cos_table.astype(jnp.float32), precision=lax.Precision.HIGHEST)
    sin_part = jnp.einsum(pattern, operand, sin_table.astype(jnp.float32), precision=lax.Precision.HIGHEST)
    return combine_halves(cos_part, sin_part)

def along_last(values, matrix):
    return jnp.einsum('abc,cd->abd', values.astype(jnp.float32), matrix.astype(jnp.float32), precision=lax.Precision.HIGHEST)

def kinetic_table(box_size, row_start, column_count):
    center = box_size // 2
    freq_rows = jnp.arange(box_size, dtype=jnp.float32) - center
    freq_cols = (row_start + jnp.arange(column_count, dtype=jnp.int32)).astype(jnp.float32) - center
    freq_depth = jnp.arange(box_size, dtype=jnp.float32) - center
    freq_depth = jnp.concatenate([freq_depth, freq_depth])
    squares = freq_rows[:, None, None] ** 2 + freq_cols[None, :, None] ** 2 + freq_depth[None, None, :] ** 2
    return 0.5 * squares / float(center * center)

def reference(wavefunctions, potential, keep_mask, stick_map):
    row_width = 2 * GBOX
    middle = GBOX
    precise = lax.Precision.HIGHEST
    slices = wavefunctions.reshape(N_CUTS, BANDS_DEV, STICKS, row_width)
    lower_edge = slices[:, :EDGE].astype(jnp.float32)
    upper_edge = slices[:, BANDS_DEV - EDGE:].astype(jnp.float32)
    neighbor = jnp.concatenate([jnp.zeros_like(upper_edge[:1]), upper_edge[:-1]], axis=0)
    correlation_real = jnp.einsum('sjgc,sigc->sji', neighbor, lower_edge, precision=precise)
    correlation_imag = jnp.einsum('sjgc,sigc->sji', neighbor[..., :middle], lower_edge[..., middle:], precision=precise) - jnp.einsum('sjgc,sigc->sji', neighbor[..., middle:], lower_edge[..., :middle], precision=precise)
    neighbor_norms = lax.optimization_barrier(jnp.sum(neighbor * neighbor, axis=(2, 3)))
    divisor = neighbor_norms[:, None, :] + 1e-05
    keep_factor = keep_mask.astype(jnp.float32)
    weight_real = keep_factor * jnp.transpose(correlation_real, (0, 2, 1)) / divisor
    weight_imag = keep_factor * jnp.transpose(correlation_imag, (0, 2, 1)) / divisor
    cos_part = jnp.einsum('sij,sjgc->sigc', weight_real, neighbor, precision=precise)
    sin_part = jnp.einsum('sij,sjgc->sigc', weight_imag, neighbor, precision=precise)
    new_lower = (lower_edge - combine_halves(cos_part, sin_part)).astype(jnp.bfloat16)
    ortho = slices.at[:, :EDGE].set(new_lower).reshape(BANDS, STICKS, row_width)
    owner_rows = jnp.arange(STICKS, dtype=jnp.int32) // STICKS_DEV
    freq_first = stick_map // GY_DEV
    freq_second = owner_rows * GY_DEV + stick_map % GY_DEV
    position = (freq_first * GBOX + freq_second).astype(jnp.int32)
    inverse = jnp.zeros((STICKS,), jnp.int32).at[position].set(jnp.arange(STICKS, dtype=jnp.int32))
    kinetic = kinetic_table(GBOX, 0, GBOX)
    ahead_cos, ahead_sin, behind_cos, behind_sin = dft_tables(GBOX, GRID)
    ahead_last = last_matrix(ahead_cos, ahead_sin)
    behind_last = last_matrix(behind_cos, behind_sin)
    doubled = jnp.concatenate([potential, potential], axis=-1)

    def one_band(band_rows):
        freq_block = band_rows[inverse].reshape(GBOX, GBOX, row_width)
        section_one = along_axis(freq_block, ahead_cos, ahead_sin, 'kyc,kn->nyc').astype(jnp.bfloat16)
        section_two = along_last(section_one, ahead_last).astype(jnp.bfloat16)
        real_space = along_axis(section_two, ahead_cos, ahead_sin, 'xkc,kn->xnc').astype(jnp.bfloat16)
        scaled = (doubled * real_space.astype(jnp.float32)).astype(jnp.bfloat16)
        back_one = along_axis(scaled, behind_cos, behind_sin, 'xnc,nk->xkc').astype(jnp.bfloat16)
        back_two = along_last(back_one, behind_last).astype(jnp.bfloat16)
        back_three = along_axis(back_two, behind_cos, behind_sin, 'nyc,nk->kyc')
        result = (back_three + kinetic * freq_block.astype(jnp.float32)).astype(jnp.bfloat16)
        return result.reshape(STICKS, row_width)[position]
    return lax.map(one_band, ortho)
```

```python
import math

import jax
import jax.numpy as jnp
import numpy as np
from jax import lax
from jax.experimental import pallas as pl
from jax.experimental.pallas import tpu as pltpu
from jax.sharding import PartitionSpec as P

EDGE = 2
VMEM_BYTES = 56 * 1024 * 1024
F32 = jnp.float32
BF16 = jnp.bfloat16


def from_behind(block, axis, distance):
    devices = range(lax.axis_size(axis))
    route = [(i - distance, i) for i in devices if i - distance in devices]
    return lax.ppermute(block, axis, route)


def dft_tables(box_size, length):
    frequency = np.arange(box_size) - box_size // 2
    points = np.arange(length)
    phases = 2.0 * math.pi / length * np.mod(frequency[:, None] * points[None, :], length)
    ahead_scale = 1.0 / math.sqrt(box_size)
    behind_scale = math.sqrt(box_size) / length
    ahead_cos = np.cos(phases) * ahead_scale
    ahead_sin = np.sin(phases) * ahead_scale
    behind_cos = np.cos(phases).T * behind_scale
    behind_sin = -np.sin(phases).T * behind_scale
    return tuple(
        jnp.asarray(t.astype(np.float32)).astype(BF16)
        for t in (ahead_cos, ahead_sin, behind_cos, behind_sin)
    )


def last_matrix(cos_table, sin_table):
    upper_rows = jnp.concatenate([cos_table, sin_table], axis=1)
    lower_rows = jnp.concatenate([-sin_table, cos_table], axis=1)
    return jnp.concatenate([upper_rows, lower_rows], axis=0)


def combine_halves(cos_part, sin_part):
    middle = cos_part.shape[-1] // 2
    real_part = cos_part[..., :middle] - sin_part[..., middle:]
    imag_part = sin_part[..., :middle] + cos_part[..., middle:]
    return jnp.concatenate([real_part, imag_part], axis=-1)


def along_axis(values, cos_table, sin_table, pattern):
    cos_part = jnp.einsum(pattern, values, cos_table, preferred_element_type=F32)
    sin_part = jnp.einsum(pattern, values, sin_table, preferred_element_type=F32)
    return combine_halves(cos_part, sin_part)


def along_last(values, matrix):
    return jnp.einsum("bxyc,cd->bxyd", values, matrix, preferred_element_type=F32)


def kinetic_table(box_size, row_start, column_count):
    center = box_size // 2
    freq_rows = jnp.arange(box_size, dtype=F32) - center
    freq_cols = (row_start + jnp.arange(column_count, dtype=jnp.int32)).astype(F32) - center
    freq_depth = jnp.arange(box_size, dtype=F32) - center
    freq_depth = jnp.concatenate([freq_depth, freq_depth])
    squares = (
        freq_rows[:, None, None] ** 2
        + freq_cols[None, :, None] ** 2
        + freq_depth[None, None, :] ** 2
    )
    return 0.5 * squares / float(center * center)


def turned(values):
    middle = values.shape[-1] // 2
    return jnp.concatenate([-values[..., middle:], values[..., :middle]], axis=-1)


def turned_rows(values):
    middle = values.shape[0] // 2
    return jnp.concatenate([-values[middle:], values[:middle]], axis=0)


def lane_block(count, parts):
    block = count // parts
    return block if count % parts == 0 and block % 128 == 0 else count


def dot(a, b):
    return jnp.dot(a, b, preferred_element_type=F32)


def params(grid_dims=1):
    return pltpu.CompilerParams(
        dimension_semantics=("arbitrary",) * grid_dims, vmem_limit_bytes=VMEM_BYTES
    )


def edge_sums_kernel(behind_ref, own_ref, out_ref):
    @pl.when(pl.program_id(0) == 0)
    def _():
        out_ref[...] = jnp.zeros_like(out_ref)

    def add(slot, values):
        rows, width = values.shape
        out_ref[slot] += jnp.sum(values.reshape(rows // 8, 8, width), axis=0)

    own = [own_ref[i].astype(F32) for i in range(EDGE)]
    for j in range(EDGE):
        behind = behind_ref[j].astype(F32)
        swapped = turned_rows(behind)
        for i in range(EDGE):
            add(j * EDGE + i, behind * own[i])
            add(EDGE * EDGE + j * EDGE + i, swapped * own[i])
        add(2 * EDGE * EDGE + j, behind * behind)


def edge_sums(neighbor, bands):
    edge, row_width, sticks_dev = neighbor.shape
    width = lane_block(sticks_dev, 6)
    slots = 2 * EDGE * EDGE + EDGE
    sums = pl.pallas_call(
        edge_sums_kernel,
        grid=(sticks_dev // width,),
        in_specs=[
            pl.BlockSpec((edge, row_width, width), lambda g: (0, 0, g)),
            pl.BlockSpec((edge, row_width, width), lambda g: (0, 0, g)),
        ],
        out_specs=pl.BlockSpec((slots, 8, width), lambda g: (0, 0, 0)),
        out_shape=jax.ShapeDtypeStruct((slots, 8, width), F32),
        compiler_params=params(),
    )(neighbor, bands)
    return jnp.sum(sums, axis=(1, 2))


def edge_weights(sums, keep_mask):
    count = EDGE * EDGE
    real = sums[:count].reshape(EDGE, EDGE)
    imag = sums[count : 2 * count].reshape(EDGE, EDGE)
    divisor = sums[2 * count :][None, :] + 1e-05
    keep = keep_mask[0].astype(F32)
    return jnp.stack([keep * real.T / divisor, keep * imag.T / divisor]).reshape(-1)


def place_kernel(weight_ref, place_ref, own_ref, behind_ref, out_ref, ortho):
    bands, _, sticks_dev = own_ref.shape
    rows = out_ref.shape[1]
    chunk = lane_block(sticks_dev, 9)
    step = pl.program_id(0)

    @pl.when(step == 0)
    def _():
        ortho[EDGE:] = own_ref[EDGE:]

        @pl.loop(0, sticks_dev // chunk)
        def _(c):
            part = pl.ds(pl.multiple_of(c * chunk, chunk), chunk)
            behind = [behind_ref[j, :, part].astype(F32) for j in range(EDGE)]
            swapped = [turned_rows(values) for values in behind]
            for i in range(EDGE):
                total = own_ref[i, :, part].astype(F32)
                for j in range(EDGE):
                    total -= weight_ref[i * EDGE + j] * behind[j]
                    total -= weight_ref[EDGE * EDGE + i * EDGE + j] * swapped[j]
                ortho[i, :, part] = total.astype(BF16)

    position = step * rows + lax.broadcasted_iota(jnp.int32, (rows, sticks_dev), 0)
    chosen = jnp.where(position == place_ref[...], 1.0, 0.0).astype(BF16)
    for b in range(bands):
        out_ref[b] = lax.dot_general(
            chosen, ortho[b], (((1,), (1,)), ((), ())), preferred_element_type=F32
        ).astype(BF16)


def place(weights, places, own, neighbor):
    bands, row_width, sticks_dev = own.shape
    steps = 4
    rows = sticks_dev // steps
    whole = lambda shape: pl.BlockSpec(shape, lambda g: (0,) * len(shape))
    return pl.pallas_call(
        place_kernel,
        grid=(steps,),
        in_specs=[
            pl.BlockSpec(memory_space=pltpu.SMEM),
            whole((1, sticks_dev)),
            whole(own.shape),
            whole(neighbor.shape),
        ],
        out_specs=pl.BlockSpec((bands, rows, row_width), lambda g: (0, g, 0)),
        out_shape=jax.ShapeDtypeStruct((bands, sticks_dev, row_width), BF16),
        scratch_shapes=[pltpu.VMEM(own.shape, BF16)],
        compiler_params=params(),
    )(weights, places.reshape(1, sticks_dev), own, neighbor)


def unplace_kernel(place_ref, rows_ref, out_ref, columns):
    bands, sticks_dev, row_width = rows_ref.shape

    @pl.when(pl.program_id(0) == 0)
    def _():
        for b in range(bands):
            columns[b * row_width : (b + 1) * row_width] = rows_ref[b].T

    width = out_ref.shape[2]
    position = lax.broadcasted_iota(jnp.int32, (sticks_dev, width), 0)
    chosen = jnp.where(position == place_ref[...], 1.0, 0.0).astype(BF16)
    result = dot(columns[...], chosen).astype(BF16)
    for b in range(bands):
        out_ref[b] = result[b * row_width : (b + 1) * row_width]


def unplace(places, values):
    bands, sticks_dev, row_width = values.shape
    width = lane_block(sticks_dev, 3)
    return pl.pallas_call(
        unplace_kernel,
        grid=(sticks_dev // width,),
        in_specs=[
            pl.BlockSpec((1, width), lambda g: (0, g)),
            pl.BlockSpec(values.shape, lambda g: (0, 0, 0)),
        ],
        out_specs=pl.BlockSpec((bands, row_width, width), lambda g: (0, 0, g)),
        out_shape=jax.ShapeDtypeStruct((bands, row_width, sticks_dev), BF16),
        scratch_shapes=[pltpu.VMEM((bands * row_width, sticks_dev), BF16)],
        compiler_params=params(),
    )(places.reshape(1, sticks_dev), values)


def first_ahead_kernel(matrix_ref, in_ref, out_ref):
    for i in range(in_ref.shape[0]):
        values = in_ref[i]
        stacked = jnp.concatenate([values, turned(values)], axis=0)
        out_ref[i] = dot(matrix_ref[...], stacked).astype(BF16)


def first_ahead(matrix, block):
    columns, box_size, row_width = block.shape
    length = matrix.shape[0]
    per_step = 12 if columns % 12 == 0 else 1
    return pl.pallas_call(
        first_ahead_kernel,
        grid=(columns // per_step,),
        in_specs=[
            pl.BlockSpec(matrix.shape, lambda g: (0, 0)),
            pl.BlockSpec((per_step, box_size, row_width), lambda g: (g, 0, 0)),
        ],
        out_specs=pl.BlockSpec((per_step, length, row_width), lambda g: (g, 0, 0)),
        out_shape=jax.ShapeDtypeStruct((columns, length, row_width), BF16),
        compiler_params=params(),
    )(matrix, block)


def first_behind_kernel(matrix_ref, in_ref, freq_ref, out_ref):
    per_step, box_size, row_width = freq_ref.shape
    center = box_size // 2
    shape = (box_size, row_width)
    gx = lax.broadcasted_iota(jnp.int32, shape, 0) - center
    gz = lax.broadcasted_iota(jnp.int32, shape, 1)
    gz = jnp.where(gz >= box_size, gz - box_size, gz) - center
    scale = 0.5 / float(center * center)
    squares = (gx * gx + gz * gz).astype(F32)
    for i in range(per_step):
        values = in_ref[i]
        stacked = jnp.concatenate([values, turned(values)], axis=0)
        gy = pl.program_id(0) * per_step + i - center
        kinetic = (squares + (gy * gy).astype(F32)) * scale
        total = dot(matrix_ref[...], stacked) + kinetic * freq_ref[i].astype(F32)
        out_ref[i] = total.astype(BF16)


def first_behind(matrix, block, freq):
    columns, length, row_width = block.shape
    box_size = matrix.shape[0]
    per_step = 12 if columns % 12 == 0 else 1
    return pl.pallas_call(
        first_behind_kernel,
        grid=(columns // per_step,),
        in_specs=[
            pl.BlockSpec(matrix.shape, lambda g: (0, 0)),
            pl.BlockSpec((per_step, length, row_width), lambda g: (g, 0, 0)),
            pl.BlockSpec((per_step, box_size, row_width), lambda g: (g, 0, 0)),
        ],
        out_specs=pl.BlockSpec((per_step, box_size, row_width), lambda g: (g, 0, 0)),
        out_shape=jax.ShapeDtypeStruct((columns, box_size, row_width), BF16),
        compiler_params=params(),
    )(matrix, block, freq)


def planes_kernel(last_re, last_im, mid_ahead, mid_behind, back_re, back_im, in_ref, pot_ref, out_ref):
    planes, box_size, row_width = in_ref.shape
    length = pot_ref.shape[-1]
    rows = in_ref[...].reshape(planes * box_size, row_width)
    real = dot(rows, last_re[...]).astype(BF16)
    imag = dot(rows, last_im[...]).astype(BF16)
    for i in range(planes):
        part = slice(i * box_size, (i + 1) * box_size)
        stacked = jnp.concatenate([real[part], imag[part]], axis=0)
        space = dot(mid_ahead[...], stacked)
        local = pot_ref[0, 0, i].astype(F32)
        scaled = jnp.concatenate(
            [(space[:length] * local).astype(BF16), (space[length:] * local).astype(BF16)], axis=0
        )
        back = dot(mid_behind[...], scaled).astype(BF16)
        out = dot(back[:box_size], back_re[...]) + dot(back[box_size:], back_im[...])
        out_ref[i] = out.astype(BF16)


def planes(matrices, block, potential):
    count, box_size, row_width = block.shape
    cuts, pencils, per_step, length, _ = potential.shape
    return pl.pallas_call(
        planes_kernel,
        grid=(count // per_step,),
        in_specs=[pl.BlockSpec(m.shape, lambda g: (0, 0)) for m in matrices]
        + [
            pl.BlockSpec((per_step, box_size, row_width), lambda g: (g, 0, 0)),
            pl.BlockSpec(
                (1, 1, per_step, length, length), lambda g: (g % cuts, g // cuts, 0, 0, 0)
            ),
        ],
        out_specs=pl.BlockSpec((per_step, box_size, row_width), lambda g: (g, 0, 0)),
        out_shape=jax.ShapeDtypeStruct(block.shape, BF16),
        compiler_params=params(),
    )(*matrices, block, potential)


def hamiltonian_whole_bands(freq_rows, potential_all, rows_local):
    bands_dev, sticks_dev, row_width = freq_rows.shape
    box_size = row_width // 2
    length = potential_all.shape[-1]
    ahead_cos, ahead_sin, behind_cos, behind_sin = dft_tables(box_size, length)
    last_ahead = last_matrix(ahead_cos, ahead_sin)
    last_behind = last_matrix(behind_cos, behind_sin)
    middle_ahead = jnp.concatenate(
        [
            jnp.concatenate([ahead_cos.T, -ahead_sin.T], axis=1),
            jnp.concatenate([ahead_sin.T, ahead_cos.T], axis=1),
        ],
        axis=0,
    )
    middle_behind = jnp.concatenate(
        [
            jnp.concatenate([behind_cos.T, -behind_sin.T], axis=1),
            jnp.concatenate([behind_sin.T, behind_cos.T], axis=1),
        ],
        axis=0,
    )
    first_a = jnp.concatenate([ahead_cos.T, ahead_sin.T], axis=1)
    first_b = jnp.concatenate([behind_cos.T, behind_sin.T], axis=1)
    matrices = (
        last_ahead[:, :length],
        last_ahead[:, length:],
        middle_ahead,
        middle_behind,
        last_behind[:length],
        last_behind[length:],
    )
    sent = freq_rows.reshape(bands_dev, rows_local, box_size, row_width)
    freq = lax.all_to_all(sent, "pencil", split_axis=0, concat_axis=0, tiled=True)
    freq = freq.reshape(bands_dev * rows_local, box_size, row_width)
    section = jnp.swapaxes(first_ahead(first_a, freq), 0, 1)
    section = planes(matrices, section, potential_all)
    result = first_behind(first_b, jnp.swapaxes(section, 0, 1), freq)
    result = result.reshape(bands_dev, rows_local, box_size, row_width)
    result = lax.all_to_all(result, "pencil", split_axis=0, concat_axis=0, tiled=True)
    return result.reshape(bands_dev, sticks_dev, row_width)


def hamiltonian_split_bands(freq_rows, potential, rows_local):
    bands_dev, sticks_dev, row_width = freq_rows.shape
    box_size = row_width // 2
    length = potential.shape[-1]
    freq_block = jnp.swapaxes(freq_rows.reshape(bands_dev, rows_local, box_size, row_width), 1, 2)
    ahead_cos, ahead_sin, behind_cos, behind_sin = dft_tables(box_size, length)
    ahead_last = last_matrix(ahead_cos, ahead_sin)
    behind_last = last_matrix(behind_cos, behind_sin)
    doubled = jnp.concatenate([potential, potential], axis=-1)
    section_one = along_axis(freq_block, ahead_cos, ahead_sin, "bkyc,kn->bnyc").astype(BF16)
    section_two = along_last(
        lax.all_to_all(section_one, "pencil", split_axis=1, concat_axis=2, tiled=True), ahead_last
    ).astype(BF16)
    real_space = along_axis(section_two, ahead_cos, ahead_sin, "bxkc,kn->bxnc").astype(BF16)
    scaled = (doubled * real_space.astype(F32)).astype(BF16)
    back_one = along_axis(scaled, behind_cos, behind_sin, "bxnc,nk->bxkc").astype(BF16)
    back_two = along_last(back_one, behind_last).astype(BF16)
    back_two = lax.all_to_all(back_two, "pencil", split_axis=2, concat_axis=1, tiled=True)
    back_three = along_axis(back_two, behind_cos, behind_sin, "bnyc,nk->bkyc")
    row_start = lax.axis_index("pencil") * rows_local
    kinetic = kinetic_table(box_size, row_start, rows_local)
    result = (back_three + kinetic * freq_block.astype(F32)).astype(BF16)
    return jnp.swapaxes(result, 1, 2).reshape(bands_dev, sticks_dev, row_width)


def local(wavefunctions, potential, keep_mask, stick_map):
    bands_dev, sticks_dev, row_width = wavefunctions.shape
    box_size = row_width // 2
    rows_local = sticks_dev // box_size
    cuts, pencils = lax.axis_size("cuts"), lax.axis_size("pencil")
    whole_bands = bands_dev == pencils and potential.shape[0] % cuts == 0
    if whole_bands:
        share = potential.shape[0] // cuts
        mine = lax.dynamic_slice_in_dim(potential, lax.axis_index("cuts") * share, share, 0)
        potential_all = lax.all_gather(mine.astype(BF16), ("cuts", "pencil"), axis=0, tiled=False)
        potential_all = potential_all.reshape((cuts, pencils) + mine.shape)
    own = jnp.swapaxes(wavefunctions, 1, 2)
    neighbor = from_behind(own[bands_dev - EDGE :], "cuts", 1)
    sums = lax.psum(edge_sums(neighbor, own), "pencil")
    weights = edge_weights(sums, keep_mask)
    places = (stick_map % rows_local) * box_size + stick_map // rows_local
    freq_rows = place(weights, places, own, neighbor)
    if whole_bands:
        result = hamiltonian_whole_bands(freq_rows, potential_all, rows_local)
    else:
        result = hamiltonian_split_bands(freq_rows, potential, rows_local)
    return jnp.swapaxes(unplace(places, result), 1, 2)


def solution(mesh):
    return jax.shard_map(
        local,
        mesh=mesh,
        in_specs=(
            P("cuts", "pencil", None),
            P("pencil", None, None),
            P("cuts", None, None),
            P("pencil"),
        ),
        out_specs=P("cuts", "pencil", None),
        check_vma=False,
    )
```

```python
import math

import jax
import jax.numpy as jnp
import numpy as np
from jax import lax
from jax.experimental import pallas as pl
from jax.experimental.pallas import tpu as pltpu
from jax.sharding import PartitionSpec as P

EDGE = 2
VMEM_BYTES = 56 * 1024 * 1024
F32 = jnp.float32
BF16 = jnp.bfloat16


def from_behind(block, axis, distance):
    devices = range(lax.axis_size(axis))
    route = [(i - distance, i) for i in devices if i - distance in devices]
    return lax.ppermute(block, axis, route)


def dft_tables(box_size, length):
    frequency = np.arange(box_size) - box_size // 2
    points = np.arange(length)
    phases = 2.0 * math.pi / length * np.mod(frequency[:, None] * points[None, :], length)
    ahead_scale = 1.0 / math.sqrt(box_size)
    behind_scale = math.sqrt(box_size) / length
    ahead_cos = np.cos(phases) * ahead_scale
    ahead_sin = np.sin(phases) * ahead_scale
    behind_cos = np.cos(phases).T * behind_scale
    behind_sin = -np.sin(phases).T * behind_scale
    return tuple(
        jnp.asarray(t.astype(np.float32)).astype(BF16)
        for t in (ahead_cos, ahead_sin, behind_cos, behind_sin)
    )


def last_matrix(cos_table, sin_table):
    upper_rows = jnp.concatenate([cos_table, sin_table], axis=1)
    lower_rows = jnp.concatenate([-sin_table, cos_table], axis=1)
    return jnp.concatenate([upper_rows, lower_rows], axis=0)


def combine_halves(cos_part, sin_part):
    middle = cos_part.shape[-1] // 2
    real_part = cos_part[..., :middle] - sin_part[..., middle:]
    imag_part = sin_part[..., :middle] + cos_part[..., middle:]
    return jnp.concatenate([real_part, imag_part], axis=-1)


def along_axis(values, cos_table, sin_table, pattern):
    cos_part = jnp.einsum(pattern, values, cos_table, preferred_element_type=F32)
    sin_part = jnp.einsum(pattern, values, sin_table, preferred_element_type=F32)
    return combine_halves(cos_part, sin_part)


def along_last(values, matrix):
    return jnp.einsum("bxyc,cd->bxyd", values, matrix, preferred_element_type=F32)


def kinetic_table(box_size, row_start, column_count):
    center = box_size // 2
    freq_rows = jnp.arange(box_size, dtype=F32) - center
    freq_cols = (row_start + jnp.arange(column_count, dtype=jnp.int32)).astype(F32) - center
    freq_depth = jnp.arange(box_size, dtype=F32) - center
    freq_depth = jnp.concatenate([freq_depth, freq_depth])
    squares = (
        freq_rows[:, None, None] ** 2
        + freq_cols[None, :, None] ** 2
        + freq_depth[None, None, :] ** 2
    )
    return 0.5 * squares / float(center * center)


def turned(values):
    middle = values.shape[-1] // 2
    return jnp.concatenate([-values[..., middle:], values[..., :middle]], axis=-1)


def turned_rows(values):
    middle = values.shape[0] // 2
    return jnp.concatenate([-values[middle:], values[:middle]], axis=0)


def lane_block(count, parts):
    block = count // parts
    return block if count % parts == 0 and block % 128 == 0 else count


def dot(a, b):
    return jnp.dot(a, b, preferred_element_type=F32)


def params(grid_dims=1):
    return pltpu.CompilerParams(
        dimension_semantics=("arbitrary",) * grid_dims, vmem_limit_bytes=VMEM_BYTES
    )


def edge_sums_kernel(behind_ref, own_ref, out_ref):
    @pl.when(pl.program_id(0) == 0)
    def _():
        out_ref[...] = jnp.zeros_like(out_ref)

    def add(slot, values):
        rows, width = values.shape
        out_ref[slot] += jnp.sum(values.reshape(rows // 8, 8, width), axis=0)

    own = [own_ref[i].astype(F32) for i in range(EDGE)]
    for j in range(EDGE):
        behind = behind_ref[j].astype(F32)
        swapped = turned_rows(behind)
        for i in range(EDGE):
            add(j * EDGE + i, behind * own[i])
            add(EDGE * EDGE + j * EDGE + i, swapped * own[i])
        add(2 * EDGE * EDGE + j, behind * behind)


def edge_sums(neighbor, bands):
    edge, row_width, sticks_dev = neighbor.shape
    width = lane_block(sticks_dev, 6)
    slots = 2 * EDGE * EDGE + EDGE
    sums = pl.pallas_call(
        edge_sums_kernel,
        grid=(sticks_dev // width,),
        in_specs=[
            pl.BlockSpec((edge, row_width, width), lambda g: (0, 0, g)),
            pl.BlockSpec((edge, row_width, width), lambda g: (0, 0, g)),
        ],
        out_specs=pl.BlockSpec((slots, 8, width), lambda g: (0, 0, 0)),
        out_shape=jax.ShapeDtypeStruct((slots, 8, width), F32),
        compiler_params=params(),
    )(neighbor, bands)
    return jnp.sum(sums, axis=(1, 2))


def edge_weights(sums, keep_mask):
    count = EDGE * EDGE
    real = sums[:count].reshape(EDGE, EDGE)
    imag = sums[count : 2 * count].reshape(EDGE, EDGE)
    divisor = sums[2 * count :][None, :] + 1e-05
    keep = keep_mask[0].astype(F32)
    return jnp.stack([keep * real.T / divisor, keep * imag.T / divisor]).reshape(-1)


def place_kernel(weight_ref, place_ref, own_ref, behind_ref, out_ref, ortho):
    bands, _, sticks_dev = own_ref.shape
    rows = out_ref.shape[1]
    chunk = lane_block(sticks_dev, 9)
    step = pl.program_id(0)

    @pl.when(step == 0)
    def _():
        ortho[EDGE:] = own_ref[EDGE:]

        @pl.loop(0, sticks_dev // chunk)
        def _(c):
            part = pl.ds(pl.multiple_of(c * chunk, chunk), chunk)
            behind = [behind_ref[j, :, part].astype(F32) for j in range(EDGE)]
            swapped = [turned_rows(values) for values in behind]
            for i in range(EDGE):
                total = own_ref[i, :, part].astype(F32)
                for j in range(EDGE):
                    total -= weight_ref[i * EDGE + j] * behind[j]
                    total -= weight_ref[EDGE * EDGE + i * EDGE + j] * swapped[j]
                ortho[i, :, part] = total.astype(BF16)

    position = step * rows + lax.broadcasted_iota(jnp.int32, (rows, sticks_dev), 0)
    chosen = jnp.where(position == place_ref[...], 1.0, 0.0).astype(BF16)
    for b in range(bands):
        out_ref[b] = lax.dot_general(
            chosen, ortho[b], (((1,), (1,)), ((), ())), preferred_element_type=F32
        ).astype(BF16)


def place(weights, places, own, neighbor):
    bands, row_width, sticks_dev = own.shape
    steps = 4
    rows = sticks_dev // steps
    whole = lambda shape: pl.BlockSpec(shape, lambda g: (0,) * len(shape))
    return pl.pallas_call(
        place_kernel,
        grid=(steps,),
        in_specs=[
            pl.BlockSpec(memory_space=pltpu.SMEM),
            whole((1, sticks_dev)),
            whole(own.shape),
            whole(neighbor.shape),
        ],
        out_specs=pl.BlockSpec((bands, rows, row_width), lambda g: (0, g, 0)),
        out_shape=jax.ShapeDtypeStruct((bands, sticks_dev, row_width), BF16),
        scratch_shapes=[pltpu.VMEM(own.shape, BF16)],
        compiler_params=params(),
    )(weights, places.reshape(1, sticks_dev), own, neighbor)


def unplace_kernel(place_ref, rows_ref, out_ref, columns):
    bands, sticks_dev, row_width = rows_ref.shape

    @pl.when(pl.program_id(0) == 0)
    def _():
        for b in range(bands):
            columns[b * row_width : (b + 1) * row_width] = rows_ref[b].T

    width = out_ref.shape[2]
    position = lax.broadcasted_iota(jnp.int32, (sticks_dev, width), 0)
    chosen = jnp.where(position == place_ref[...], 1.0, 0.0).astype(BF16)
    result = dot(columns[...], chosen).astype(BF16)
    for b in range(bands):
        out_ref[b] = result[b * row_width : (b + 1) * row_width]


def unplace(places, values):
    bands, sticks_dev, row_width = values.shape
    width = lane_block(sticks_dev, 3)
    return pl.pallas_call(
        unplace_kernel,
        grid=(sticks_dev // width,),
        in_specs=[
            pl.BlockSpec((1, width), lambda g: (0, g)),
            pl.BlockSpec(values.shape, lambda g: (0, 0, 0)),
        ],
        out_specs=pl.BlockSpec((bands, row_width, width), lambda g: (0, 0, g)),
        out_shape=jax.ShapeDtypeStruct((bands, row_width, sticks_dev), BF16),
        scratch_shapes=[pltpu.VMEM((bands * row_width, sticks_dev), BF16)],
        compiler_params=params(),
    )(places.reshape(1, sticks_dev), values)


def first_ahead_kernel(matrix_ref, in_ref, out_ref):
    for i in range(in_ref.shape[0]):
        values = in_ref[i]
        stacked = jnp.concatenate([values, turned(values)], axis=0)
        out_ref[i] = dot(matrix_ref[...], stacked).astype(BF16)


def first_ahead(matrix, block):
    columns, box_size, row_width = block.shape
    length = matrix.shape[0]
    per_step = 12 if columns % 12 == 0 else 1
    return pl.pallas_call(
        first_ahead_kernel,
        grid=(columns // per_step,),
        in_specs=[
            pl.BlockSpec(matrix.shape, lambda g: (0, 0)),
            pl.BlockSpec((per_step, box_size, row_width), lambda g: (g, 0, 0)),
        ],
        out_specs=pl.BlockSpec((per_step, length, row_width), lambda g: (g, 0, 0)),
        out_shape=jax.ShapeDtypeStruct((columns, length, row_width), BF16),
        compiler_params=params(),
    )(matrix, block)


def first_behind_kernel(matrix_ref, in_ref, freq_ref, out_ref):
    per_step, box_size, row_width = freq_ref.shape
    center = box_size // 2
    shape = (box_size, row_width)
    gx = lax.broadcasted_iota(jnp.int32, shape, 0) - center
    gz = lax.broadcasted_iota(jnp.int32, shape, 1)
    gz = jnp.where(gz >= box_size, gz - box_size, gz) - center
    scale = 0.5 / float(center * center)
    squares = (gx * gx + gz * gz).astype(F32)
    for i in range(per_step):
        values = in_ref[i]
        stacked = jnp.concatenate([values, turned(values)], axis=0)
        gy = pl.program_id(0) * per_step + i - center
        kinetic = (squares + (gy * gy).astype(F32)) * scale
        total = dot(matrix_ref[...], stacked) + kinetic * freq_ref[i].astype(F32)
        out_ref[i] = total.astype(BF16)


def first_behind(matrix, block, freq):
    columns, length, row_width = block.shape
    box_size = matrix.shape[0]
    per_step = 12 if columns % 12 == 0 else 1
    return pl.pallas_call(
        first_behind_kernel,
        grid=(columns // per_step,),
        in_specs=[
            pl.BlockSpec(matrix.shape, lambda g: (0, 0)),
            pl.BlockSpec((per_step, length, row_width), lambda g: (g, 0, 0)),
            pl.BlockSpec((per_step, box_size, row_width), lambda g: (g, 0, 0)),
        ],
        out_specs=pl.BlockSpec((per_step, box_size, row_width), lambda g: (g, 0, 0)),
        out_shape=jax.ShapeDtypeStruct((columns, box_size, row_width), BF16),
        compiler_params=params(),
    )(matrix, block, freq)


def planes_kernel(last_re, last_im, mid_ahead, mid_behind, back_re, back_im, in_ref, pot_ref, out_ref):
    planes, box_size, row_width = in_ref.shape
    length = pot_ref.shape[-1]
    rows = in_ref[...].reshape(planes * box_size, row_width)
    real = dot(rows, last_re[...]).astype(BF16)
    imag = dot(rows, last_im[...]).astype(BF16)
    backs = []
    for i in range(planes):
        part = slice(i * box_size, (i + 1) * box_size)
        stacked = jnp.concatenate([real[part], imag[part]], axis=0)
        space = dot(mid_ahead[...], stacked)
        local = pot_ref[0, 0, i].astype(F32)
        scaled = jnp.concatenate(
            [(space[:length] * local).astype(BF16), (space[length:] * local).astype(BF16)], axis=0
        )
        back = dot(mid_behind[...], scaled).astype(BF16)
        backs.append(back)
    back_rows = jnp.concatenate([back[:box_size] for back in backs], axis=0)
    back_turns = jnp.concatenate([back[box_size:] for back in backs], axis=0)
    out = dot(back_rows, back_re[...]) + dot(back_turns, back_im[...])
    out_ref[...] = out.astype(BF16).reshape(planes, box_size, row_width)


def planes(matrices, block, potential):
    count, box_size, row_width = block.shape
    cuts, pencils, per_step, length, _ = potential.shape
    return pl.pallas_call(
        planes_kernel,
        grid=(count // per_step,),
        in_specs=[pl.BlockSpec(m.shape, lambda g: (0, 0)) for m in matrices]
        + [
            pl.BlockSpec((per_step, box_size, row_width), lambda g: (g, 0, 0)),
            pl.BlockSpec(
                (1, 1, per_step, length, length), lambda g: (g % cuts, g // cuts, 0, 0, 0)
            ),
        ],
        out_specs=pl.BlockSpec((per_step, box_size, row_width), lambda g: (g, 0, 0)),
        out_shape=jax.ShapeDtypeStruct(block.shape, BF16),
        compiler_params=params(),
    )(*matrices, block, potential)


def hamiltonian_whole_bands(freq_rows, potential_all, rows_local):
    bands_dev, sticks_dev, row_width = freq_rows.shape
    box_size = row_width // 2
    length = potential_all.shape[-1]
    ahead_cos, ahead_sin, behind_cos, behind_sin = dft_tables(box_size, length)
    last_ahead = last_matrix(ahead_cos, ahead_sin)
    last_behind = last_matrix(behind_cos, behind_sin)
    middle_ahead = jnp.concatenate(
        [
            jnp.concatenate([ahead_cos.T, -ahead_sin.T], axis=1),
            jnp.concatenate([ahead_sin.T, ahead_cos.T], axis=1),
        ],
        axis=0,
    )
    middle_behind = jnp.concatenate(
        [
            jnp.concatenate([behind_cos.T, -behind_sin.T], axis=1),
            jnp.concatenate([behind_sin.T, behind_cos.T], axis=1),
        ],
        axis=0,
    )
    first_a = jnp.concatenate([ahead_cos.T, ahead_sin.T], axis=1)
    first_b = jnp.concatenate([behind_cos.T, behind_sin.T], axis=1)
    matrices = (
        last_ahead[:, :length],
        last_ahead[:, length:],
        middle_ahead,
        middle_behind,
        last_behind[:length],
        last_behind[length:],
    )
    sent = freq_rows.reshape(bands_dev, rows_local, box_size, row_width)
    freq = lax.all_to_all(sent, "pencil", split_axis=0, concat_axis=0, tiled=True)
    freq = freq.reshape(bands_dev * rows_local, box_size, row_width)
    section = jnp.swapaxes(first_ahead(first_a, freq), 0, 1)
    section = planes(matrices, section, potential_all)
    result = first_behind(first_b, jnp.swapaxes(section, 0, 1), freq)
    result = result.reshape(bands_dev, rows_local, box_size, row_width)
    result = lax.all_to_all(result, "pencil", split_axis=0, concat_axis=0, tiled=True)
    return result.reshape(bands_dev, sticks_dev, row_width)


def hamiltonian_split_bands(freq_rows, potential, rows_local):
    bands_dev, sticks_dev, row_width = freq_rows.shape
    box_size = row_width // 2
    length = potential.shape[-1]
    freq_block = jnp.swapaxes(freq_rows.reshape(bands_dev, rows_local, box_size, row_width), 1, 2)
    ahead_cos, ahead_sin, behind_cos, behind_sin = dft_tables(box_size, length)
    ahead_last = last_matrix(ahead_cos, ahead_sin)
    behind_last = last_matrix(behind_cos, behind_sin)
    doubled = jnp.concatenate([potential, potential], axis=-1)
    section_one = along_axis(freq_block, ahead_cos, ahead_sin, "bkyc,kn->bnyc").astype(BF16)
    section_two = along_last(
        lax.all_to_all(section_one, "pencil", split_axis=1, concat_axis=2, tiled=True), ahead_last
    ).astype(BF16)
    real_space = along_axis(section_two, ahead_cos, ahead_sin, "bxkc,kn->bxnc").astype(BF16)
    scaled = (doubled * real_space.astype(F32)).astype(BF16)
    back_one = along_axis(scaled, behind_cos, behind_sin, "bxnc,nk->bxkc").astype(BF16)
    back_two = along_last(back_one, behind_last).astype(BF16)
    back_two = lax.all_to_all(back_two, "pencil", split_axis=2, concat_axis=1, tiled=True)
    back_three = along_axis(back_two, behind_cos, behind_sin, "bnyc,nk->bkyc")
    row_start = lax.axis_index("pencil") * rows_local
    kinetic = kinetic_table(box_size, row_start, rows_local)
    result = (back_three + kinetic * freq_block.astype(F32)).astype(BF16)
    return jnp.swapaxes(result, 1, 2).reshape(bands_dev, sticks_dev, row_width)


def local(wavefunctions, potential, keep_mask, stick_map):
    bands_dev, sticks_dev, row_width = wavefunctions.shape
    box_size = row_width // 2
    rows_local = sticks_dev // box_size
    cuts, pencils = lax.axis_size("cuts"), lax.axis_size("pencil")
    whole_bands = bands_dev == pencils and potential.shape[0] % cuts == 0
    if whole_bands:
        share = potential.shape[0] // cuts
        mine = lax.dynamic_slice_in_dim(potential, lax.axis_index("cuts") * share, share, 0)
        shares = lax.all_gather(mine.astype(BF16), "pencil", axis=0, tiled=False)
    own = jnp.swapaxes(wavefunctions, 1, 2)
    neighbor = from_behind(own[bands_dev - EDGE :], "cuts", 1)
    sums = edge_sums(neighbor, own)
    if whole_bands:
        shares, sums = lax.optimization_barrier((shares, sums))
        potential_all = lax.all_gather(shares, "cuts", axis=0, tiled=False)
    sums = lax.psum(sums, "pencil")
    weights = edge_weights(sums, keep_mask)
    places = (stick_map % rows_local) * box_size + stick_map // rows_local
    freq_rows = place(weights, places, own, neighbor)
    if whole_bands:
        result = hamiltonian_whole_bands(freq_rows, potential_all, rows_local)
    else:
        result = hamiltonian_split_bands(freq_rows, potential, rows_local)
    return jnp.swapaxes(unplace(places, result), 1, 2)


def solution(mesh):
    return jax.shard_map(
        local,
        mesh=mesh,
        in_specs=(
            P("cuts", "pencil", None),
            P("pencil", None, None),
            P("cuts", None, None),
            P("pencil"),
        ),
        out_specs=P("cuts", "pencil", None),
        check_vma=False,
    )
```
